32 devices in a mesh: ens: 2 (over x), tile: 16 (over z, y, core).
Axes of the slice: x: 2, y: 2, z: 4, core: 2. Of those that a mesh axis runs over, the one named last changes fastest.
Arguments:
- atmosphere: bfloat16 [256, 256, 128], P(('ens', 'tile')), parts along dimension 0, may hold values from -6 to 6
- ocean_state: bfloat16 [4096, 512], P(('ens', 'tile')), parts along dimension 0, may hold values from -6 to 6
- land_sea: int32 [2048], P('tile'), may hold values 0 or 1
- owners: int32 [2048, 1], P('tile'), may hold values from 0 to 15; in each aligned block of 128 rows (0 to 127, 128 to 255, ...) at most 16 rows name the same one
- rotations: int32 [16], replicated, may hold values from 0 to 255
- conv_weight: bfloat16 [3, 9, 128, 128], replicated, may hold values from -0.1875 to 0.1875
- conv_bias: bfloat16 [3, 128], replicated, may hold values from -3 to 3
- force_weight: bfloat16 [128, 32], replicated, may hold values from -0.5 to 0.5
- ocean_weight: bfloat16 [16, 9, 64, 32], P('tile'), may hold values from -0.25 to 0.25
Outputs:
- atmos_out: bfloat16 [256, 256, 128], P(('ens', 'tile')), parts along dimension 0
- sea_state: bfloat16 [4096, 512], P(('ens', 'tile')), parts along dimension 0
The draws below stay inside these ranges and needn't reach their ends.
There are 2 independent parts, one for each index of `ens`. The reference program is written for one: setup_inputs(seed, part) draws one part's arguments, and reference() takes and returns one part's arrays. A program takes and returns all parts, laid end to end along the dimension named above; an argument that names none is the same for every part. Nothing has to cross between parts.
Inputs may be any that keep to these rules, and one draw needn't show every extreme that they name: `owners`: among the 128 blocks of one band no owner appears more than 16 times, and some owner appears exactly 16 times.
All inputs are finite; a program needn't handle non-finite values. No bound on the sum of `land_sea` on one device may be relied on, other than what follows from the above.
Results may differ from the reference program's by a relative error of at most 0.009.
Values may be sent and summed in bfloat16 or wider, within the bound.
A program may use at most 64 MiB of HBM per device.

```python
import math
import jax
import jax.numpy as jnp
import numpy as np
from jax import lax

C = 128
OC = 32
BR = 8
LON = 256
LEADS = 2
LAYERS = 3
BH = 4
BW = 4
TILES = 16
ROWS = 128
NB = 128
BLOCKS = 2048
BLK = 512
CAP = 16


def set_ends(array, key, smallest, high):
    dims = array.shape
    index_at = [jax.random.randint(jax.random.fold_in(key, axis), (), 0, dims[axis]) for axis in range(len(dims))]
    array = array.at[tuple(index_at)].set(smallest)
    longest = dims.index(max(dims))
    index_at[longest] = (index_at[longest] + 1) % dims[longest]
    return array.at[tuple(index_at)].set(high)


def steps_of(stream_key, dims, cuts, smallest, high):
    def one(position, blocks):
        draws = jax.random.uniform(jax.random.fold_in(jax.random.fold_in(stream_key, 6), position), (blocks,), jnp.float32, smallest / len(cuts), high / len(cuts))
        return jnp.repeat(jnp.exp(draws), dims[position] // blocks).reshape((-1,) + (1,) * (len(dims) - position - 1))

    level = one(*cuts[0])
    for cut in cuts[1:]:
        level = level * one(*cut)
    return level


def deal_out(key, own, number, rows, number_of, top, bound, lean):
    sequence = jax.random.permutation(key, number_of)
    crowded, usual = shares(number_of, rows * top, bound, lean, True), shares(number_of, rows * top, bound, lean, False)
    places = jnp.arange(number_of)

    def named(tallies, offset_by):
        used = int((tallies > 0).sum())
        fixed = max(1, used // 4)
        passed = fixed + (places - fixed + offset_by * (used - fixed)) % max(1, number_of - fixed)
        return jnp.zeros((number_of,), jnp.int32).at[sequence[jnp.where(places < fixed, places, passed)]].set(jnp.asarray(tallies, jnp.int32))

    tallies = jnp.where(number % 4 == 0, named(crowded, number // 4), named(usual, number - number // 4 - 1))
    mixed = jax.random.permutation(jax.random.fold_in(own, 3), number_of)
    source_of, sink = mixed[0:number_of // 2 * 2:2], mixed[1:number_of // 2 * 2:2]
    room = jnp.minimum(tallies[source_of] - 1, bound - tallies[sink]) // 2
    room = jnp.where((source_of == sequence[0]) | (sink == sequence[0]) | (tallies[sink] == 0), 0, jnp.maximum(room, 0))
    passed = jax.random.randint(jax.random.fold_in(own, 4), (number_of // 2,), 0, 1 << 20) % (room + 1)
    tallies = tallies.at[source_of].add(-passed).at[sink].add(passed)
    labels = jnp.searchsorted(jnp.cumsum(tallies), jnp.arange(rows * top), side="right").astype(jnp.int32)
    table = labels.reshape(top, rows).T
    table = table[jax.random.permutation(jax.random.fold_in(own, 1), rows)]
    offset_by = jax.random.randint(jax.random.fold_in(own, 2), (rows, 1), 0, top)
    return jnp.take_along_axis(table, (jnp.arange(top)[None, :] + offset_by) % top, axis=1)


def shares(number_of, total, bound, lean, full):
    weights = [(1 << 20) // math.isqrt(rank ** lean) + 1 for rank in range(1, number_of + 1)]
    largest = bound if full else min(bound, max(-(-total // number_of), total * weights[0] // sum(weights)))
    least = 1 if total - largest >= number_of - 1 else 0
    holding, spare = [largest] + [least] * (number_of - 1), total - largest - least * (number_of - 1)
    while spare > 0:
        movable = [i for i in range(1, number_of) if holding[i] < largest] or [i for i in range(1, number_of) if holding[i] < bound]
        whole, budget = sum([weights[i] for i in movable]), spare
        for i in movable:
            more = min(bound - holding[i], max(1, budget * weights[i] // whole), spare)
            holding[i] = holding[i] + more
            spare = spare - more
    return np.array(holding)


def normal_values(key, extent, deviation, reach, cuts=(), kind=jnp.bfloat16):
    values = jax.random.normal(key, extent, jnp.float32) * deviation
    if len(cuts) > 0:
        values = steps_of(key, extent, cuts, -0.22, 0.18) * values
    return jnp.clip(values, min=-reach, max=reach).astype(kind)


def setup_inputs(seed: int = 0, part: int = 0) -> dict:
    seeds = jax.random.split(jax.random.key(seed), 10)
    part_splits = jax.random.split(jax.random.fold_in(seeds[9], part), 10)
    atmosphere = normal_values(part_splits[0], (ROWS, LON, C), 1.0, 6.0, ((0, 16),))
    ocean_state = normal_values(part_splits[1], (BLOCKS, BLK), 1.0, 6.0, ((0, 16),))
    land_sea = set_ends((jax.random.randint(seeds[2], (BLOCKS,), 0, 4) < 3).astype(jnp.int32), jax.random.fold_in(seeds[2], 1), 0, 1)
    owners_keys = jax.random.split(jax.random.fold_in(seeds[3], 1), BLOCKS // NB)
    owners_turns = jax.random.permutation(jax.random.fold_in(seeds[3], 3), BLOCKS // NB)
    owners = jax.vmap(lambda own, number: deal_out(jax.random.fold_in(seeds[3], 2), own, number, NB, TILES, 1, CAP, 2))(owners_keys, owners_turns).reshape((BLOCKS, 1))
    rotations = set_ends(jax.random.randint(seeds[4], (TILES,), 0, LON), jax.random.fold_in(seeds[4], 1), 0, LON - 1).astype(jnp.int32)
    conv_weight = normal_values(seeds[5], (LAYERS, 9, C, C), (9 * C) ** -0.5, 0.1875)
    conv_bias = normal_values(seeds[6], (LAYERS, C), 0.5, 3.0)
    force_weight = normal_values(seeds[7], (C, OC), C ** -0.5, 0.5)
    ocean_weight = normal_values(seeds[8], (TILES, 9, 2 * OC, OC), (18 * OC) ** -0.5, 0.25, ((0, 16),))
    return {"atmosphere": atmosphere, "ocean_state": ocean_state, "land_sea": land_sea, "owners": owners, "rotations": rotations, "conv_weight": conv_weight, "conv_bias": conv_bias, "force_weight": force_weight, "ocean_weight": ocean_weight}


def roll_one(band_rows, amount):
    return jnp.roll(band_rows, amount, axis=1)


def reference(atmosphere, ocean_state, land_sea, owners, rotations, conv_weight, conv_bias, force_weight, ocean_weight):
    channels = atmosphere.shape[2]
    ocean_ch = force_weight.shape[1]
    bands = atmosphere.reshape(TILES, BR, LON, channels)
    current = jax.vmap(roll_one)(bands, rotations).reshape(ROWS, LON, channels)
    outputs = []
    for lead_step in range(LEADS):
        for layer_index in range(LAYERS):
            dilation = 2 ** layer_index
            wrapped = jnp.concatenate([current[:, LON - dilation:], current, current[:, :dilation]], axis=1).astype(jnp.float32)
            kernel = conv_weight[layer_index].astype(jnp.float32).reshape(3, 3, channels, channels)
            convolved = lax.conv_general_dilated(
                wrapped[None], kernel, (1, 1), ((dilation, dilation), (0, 0)),
                rhs_dilation=(dilation, dilation),
                dimension_numbers=("NHWC", "HWIO", "NHWC"),
                precision=lax.Precision.HIGHEST)[0]
            current = (current.astype(jnp.float32) + jax.nn.gelu(convolved + conv_bias[layer_index].astype(jnp.float32))).astype(jnp.bfloat16)
        stored = jax.vmap(roll_one)(current.reshape(TILES, BR, LON, channels), -rotations)
        outputs.append(stored)
    atmos_out = outputs[-1].reshape(ROWS, LON, channels)
    summed = jnp.zeros((TILES * BR * LON, ocean_ch), jnp.float32)
    for stored in outputs:
        summed = summed + jnp.dot(stored.reshape(-1, channels), force_weight, preferred_element_type=jnp.float32)
    forcing = (0.5 * summed).astype(jnp.bfloat16)
    forcing = forcing.reshape(TILES, BR // BH, BH, LON // BW, BW, ocean_ch).transpose(0, 1, 3, 5, 2, 4)
    forcing = forcing.reshape(TILES, NB, ocean_ch, BH, BW)
    state_groups = ocean_state.reshape(TILES, NB, ocean_ch, BH, BW)
    owner_groups = owners.reshape(TILES, NB).astype(jnp.int32)
    sea_groups = land_sea.reshape(TILES, NB)

    def ocean_tile(pieces):
        forcing_blocks, state_blocks, owner_list, sea_flag = pieces
        kernels = ocean_weight[owner_list].astype(jnp.float32)
        joined = jnp.concatenate([forcing_blocks, state_blocks], axis=1).astype(jnp.float32)
        padded = jnp.pad(joined, ((0, 0), (0, 0), (1, 1), (1, 1)))
        total_sum = jnp.zeros((NB, ocean_ch, BH, BW), jnp.float32)
        for tap_row in range(3):
            for tap_col in range(3):
                window = padded[:, :, tap_row:tap_row + BH, tap_col:tap_col + BW]
                total_sum = total_sum + jnp.einsum("bcij,bco->boij", window, kernels[:, tap_row * 3 + tap_col], precision=lax.Precision.HIGHEST)
        updated = (state_blocks.astype(jnp.float32) + jax.nn.gelu(total_sum)).astype(jnp.bfloat16)
        updated = jnp.where(sea_flag[:, None, None, None] > 0, updated, jnp.zeros_like(updated))
        return updated.reshape(NB, ocean_ch * BH * BW)

    sea_state = lax.map(ocean_tile, (forcing, state_groups, owner_groups, sea_groups))
    return atmos_out, sea_state.reshape(BLOCKS, BLK)
```

```python
import functools
import jax
import jax.numpy as jnp
from jax import lax
from jax.experimental import pallas as pl
from jax.experimental.pallas import tpu as pltpu
from jax.sharding import PartitionSpec as P

LEADS = 2
LAYERS = 3
BH = 4
BW = 4
MARGIN = 2**LAYERS - 1
VMEM_LIMIT = 48 * 1024 * 1024


def one_hot(mask):
    return jnp.where(mask, 1.0, 0.0).astype(jnp.bfloat16)


def moved(matrix, values):
    return jnp.dot(matrix, values, preferred_element_type=jnp.float32).astype(jnp.bfloat16)


def atmosphere_kernel(
    tile_count, rot_ref, band_ref, w_ref, bias_ref, lead1_ref, lead2_ref,
    ext, mid1, mid2, taps, send_sem, recv_sem,
):
    me = lax.axis_index("tile")
    rows, columns, channels = band_ref.shape
    has_up = me > 0
    has_down = me < tile_count - 1
    barrier = pltpu.get_barrier_semaphore()

    @pl.when(has_up)
    def _():
        pl.semaphore_signal(barrier, inc=1, device_id={"tile": me - 1})

    @pl.when(has_down)
    def _():
        pl.semaphore_signal(barrier, inc=1, device_id={"tile": me + 1})

    shift = rot_ref[me]
    to = lax.broadcasted_iota(jnp.int32, (columns, columns), 0)
    source = lax.broadcasted_iota(jnp.int32, (columns, columns), 1)
    distance = source - to + shift
    turn = one_hot((distance == 0) | (distance == columns))
    for r in range(rows):
        ext[0, MARGIN + r] = moved(turn, band_ref[r])

    pl.semaphore_wait(barrier, jnp.minimum(me, 1) + jnp.minimum(tile_count - 1 - me, 1))

    def copies(lead):
        up = pltpu.make_async_remote_copy(
            src_ref=ext.at[lead, pl.ds(MARGIN, MARGIN)],
            dst_ref=ext.at[lead, pl.ds(MARGIN + rows, MARGIN)],
            send_sem=send_sem.at[lead, 0],
            recv_sem=recv_sem.at[lead, 0],
            device_id={"tile": me - 1},
        )
        down = pltpu.make_async_remote_copy(
            src_ref=ext.at[lead, pl.ds(rows, MARGIN)],
            dst_ref=ext.at[lead, pl.ds(0, MARGIN)],
            send_sem=send_sem.at[lead, 1],
            recv_sem=recv_sem.at[lead, 1],
            device_id={"tile": me + 1},
        )
        return up, down

    def start(lead):
        up, down = copies(lead)

        @pl.when(has_up)
        def _():
            up.start()

        @pl.when(has_down)
        def _():
            down.start()

    def finish(lead):
        up, down = copies(lead)

        @pl.when(has_up)
        def _():
            down.wait_recv()

        @pl.when(has_down)
        def _():
            up.wait_recv()

    def layer(index, source_of, store, out_rows, margin_left):
        dilation = 2**index
        bias = bias_ref[pl.ds(index, 1), :].astype(jnp.float32)

        def pair(g, carry):
            r = (g // dilation) * (2 * dilation) + g % dilation
            lhs = jnp.concatenate([source_of(r + k * dilation) for k in range(4)], axis=1)
            y = jnp.dot(lhs, taps[index], preferred_element_type=jnp.float32)
            for o in range(2):
                base = o * 3 * channels
                total = (
                    pltpu.roll(y[:, base : base + channels], dilation, 0)
                    + y[:, base + channels : base + 2 * channels]
                    + pltpu.roll(
                        y[:, base + 2 * channels : base + 3 * channels], columns - dilation, 0
                    )
                )
                row = r + o * dilation
                centre = lhs[:, (1 + o) * channels : (2 + o) * channels].astype(jnp.float32)
                value = centre + jax.nn.gelu(total + bias)
                if margin_left:
                    position = me * rows - margin_left + row
                    inside = (position >= 0) & (position < tile_count * rows)
                    value = jnp.where(inside, value, 0.0)
                store(row, value.astype(jnp.bfloat16))
            return carry

        lax.fori_loop(0, out_rows // 2, pair, 0, unroll=2)

    start(0)

    for index in range(LAYERS):
        for k in range(4):
            for o in range(2):
                for b in range(3):
                    a = k - o
                    where = (
                        index,
                        pl.ds(k * channels, channels),
                        pl.ds((o * 3 + b) * channels, channels),
                    )
                    if 0 <= a <= 2:
                        taps[where] = w_ref[index, a * 3 + b]
                    else:
                        taps[where] = jnp.zeros((channels, channels), jnp.bfloat16)

    @pl.when(jnp.logical_not(has_up))
    def _():
        for lead in range(LEADS):
            for r in range(MARGIN):
                ext[lead, r] = jnp.zeros((columns, channels), jnp.bfloat16)

    @pl.when(jnp.logical_not(has_down))
    def _():
        for lead in range(LEADS):
            for r in range(MARGIN):
                ext[lead, MARGIN + rows + r] = jnp.zeros((columns, channels), jnp.bfloat16)

    def set_mid1(row, value):
        mid1[row] = value

    def set_mid2(row, value):
        mid2[row] = value

    def set_lead1(row, value):
        lead1_ref[row] = value
        ext[1, MARGIN + row] = value

    def set_lead2(row, value):
        lead2_ref[row] = value

    for lead in range(LEADS):
        finish(lead)
        layer(0, lambda r, lead=lead: ext[lead, r], set_mid1, rows + 12, 6)
        layer(1, lambda r: mid1[r], set_mid2, rows + 8, 4)
        layer(2, lambda r: mid2[r], (set_lead1, set_lead2)[lead], rows, 0)
        if lead + 1 < LEADS:
            start(lead + 1)

    for lead in range(LEADS):
        up, down = copies(lead)

        @pl.when(has_up)
        def _():
            up.wait_send()

        @pl.when(has_down)
        def _():
            down.wait_send()


def atmosphere_leads(tile_count, rotations, band, conv_weight, conv_bias):
    rows, columns, channels = band.shape
    vmem = pl.BlockSpec(memory_space=pltpu.VMEM)
    extended = (rows + 2 * MARGIN, columns, channels)
    return pl.pallas_call(
        functools.partial(atmosphere_kernel, tile_count),
        out_shape=[jax.ShapeDtypeStruct(band.shape, jnp.bfloat16)] * 2,
        in_specs=[pl.BlockSpec(memory_space=pltpu.SMEM), vmem, vmem, vmem],
        out_specs=[vmem, vmem],
        scratch_shapes=[
            pltpu.VMEM((LEADS, *extended), jnp.bfloat16),
            pltpu.VMEM((rows + 12, columns, channels), jnp.bfloat16),
            pltpu.VMEM((rows + 8, columns, channels), jnp.bfloat16),
            pltpu.VMEM((LAYERS, 4 * channels, 6 * channels), jnp.bfloat16),
            pltpu.SemaphoreType.DMA((LEADS, 2)),
            pltpu.SemaphoreType.DMA((LEADS, 2)),
        ],
        compiler_params=pltpu.CompilerParams(
            collective_id=0, has_side_effects=True, vmem_limit_bytes=VMEM_LIMIT
        ),
        cost_estimate=pl.CostEstimate(
            flops=2 * 88 * columns * 9 * channels * channels,
            bytes_accessed=4 * rows * columns * channels * 2,
            transcendentals=88 * columns * channels,
        ),
        name="atmosphere",
    )(rotations, band, conv_weight, conv_bias)


def ocean_kernel(
    tile_count, rot_ref, lead1_ref, lead2_ref, state_ref, land_ref, owner_ref, fw_ref, v_ref,
    atmos_ref, sea_ref, lhs, rhs, total,
):
    me = lax.axis_index("tile")
    rows, columns, channels = lead1_ref.shape
    blocks, width = state_ref.shape
    ocean_ch = fw_ref.shape[1]
    cells = BH * BW
    group = BW * ocean_ch
    across = columns // BW
    shift = rot_ref[me]

    to = lax.broadcasted_iota(jnp.int32, (columns, columns), 0)
    source = lax.broadcasted_iota(jnp.int32, (columns, columns), 1)
    distance = to + shift - source
    back = one_hot((distance == 0) | (distance == columns))
    for r in range(rows):
        atmos_ref[r] = moved(back, lead2_ref[r])

    distance = (to % across) * BW + to // across + shift - source
    gather = one_hot((distance == 0) | (distance == columns))
    lane = lax.broadcasted_iota(jnp.int32, (ocean_ch, group), 1)
    spread = one_hot(lane % ocean_ch == lax.broadcasted_iota(jnp.int32, (ocean_ch, group), 0))
    fw4 = moved(fw_ref[...], spread)

    s = lax.broadcasted_iota(jnp.int32, (width, width), 0)
    t = lax.broadcasted_iota(jnp.int32, (width, width), 1)
    permute = one_hot((s // cells == t % ocean_ch) & (s % cells == t // ocean_ch))
    state = moved(state_ref[...], permute)

    piece_lane = lax.broadcasted_iota(jnp.int32, (across, group), 1) // ocean_ch
    lhs[...] = jnp.zeros_like(lhs)
    wide = 2 * group
    for r in range(rows):
        i, pr = r // BH, r % BH
        forcing = 0.5 * (
            jnp.dot(lead1_ref[r], fw4, preferred_element_type=jnp.float32)
            + jnp.dot(lead2_ref[r], fw4, preferred_element_type=jnp.float32)
        )
        y = jnp.dot(gather, forcing.astype(jnp.bfloat16), preferred_element_type=jnp.float32)
        piece = jnp.zeros((across, group), jnp.float32)
        for pc in range(BW):
            piece = jnp.where(piece_lane == pc, y[pc * across : (pc + 1) * across], piece)
        piece = piece.astype(jnp.bfloat16)
        for a in range(3):
            q = pr + 1 - a
            if 0 <= q < BH:
                lhs[pl.ds(q * blocks + i * across, across), pl.ds(a * wide, group)] = piece
    for pr in range(BH):
        for a in range(3):
            q = pr + 1 - a
            if 0 <= q < BH:
                lhs[pl.ds(q * blocks, blocks), pl.ds(a * wide + group, group)] = state[
                    :, pr * group : (pr + 1) * group
                ]

    owner = jnp.concatenate([jnp.broadcast_to(owner_ref[...], (blocks, group))] * BH, axis=0)
    total[...] = jnp.zeros_like(total)
    v_lane = lax.broadcasted_iota(jnp.int32, (v_ref.shape[1], group), 1) // ocean_ch

    def two_owners(k, carry):
        for half in range(2):
            v = v_ref[2 * k + half].astype(jnp.float32)
            for pc in range(BW):
                turned = v if pc == 1 else pltpu.roll(v, ((pc - 1) * ocean_ch) % group, 1)
                if pc == 0:
                    turned = jnp.where(v_lane == BW - 1, 0.0, turned)
                if pc > 2:
                    turned = jnp.where(v_lane < pc - 1, 0.0, turned)
                turned = turned.astype(jnp.bfloat16)
                for ah in range(6):
                    rhs[
                        pl.ds(ah * group + pc * ocean_ch, ocean_ch), pl.ds(half * group, group)
                    ] = turned[ah * ocean_ch : (ah + 1) * ocean_ch]
        y = jnp.dot(lhs[...], rhs[...], preferred_element_type=jnp.float32)
        kept = jnp.where(owner == 2 * k, y[:, :group], total[...])
        total[...] = jnp.where(owner == 2 * k + 1, y[:, group:], kept)
        return carry

    lax.fori_loop(0, tile_count // 2, two_owners, 0)

    sea = jnp.broadcast_to(land_ref[...], (blocks, group)) > 0
    out = jnp.zeros((blocks, width), jnp.float32)
    t = lax.broadcasted_iota(jnp.int32, (group, width), 0)
    s = lax.broadcasted_iota(jnp.int32, (group, width), 1)
    for q in range(BH):
        old = state[:, q * group : (q + 1) * group].astype(jnp.float32)
        new = old + jax.nn.gelu(total[pl.ds(q * blocks, blocks), :])
        new = jnp.where(sea, new, 0.0).astype(jnp.bfloat16)
        tq = t + q * group
        unpermute = one_hot((s // cells == tq % ocean_ch) & (s % cells == tq // ocean_ch))
        out = out + jnp.dot(new, unpermute, preferred_element_type=jnp.float32)
    sea_ref[...] = out.astype(jnp.bfloat16)


def ocean_step(tile_count, rotations, lead1, lead2, state, land, owners, force_weight, gathered):
    vmem = pl.BlockSpec(memory_space=pltpu.VMEM)
    blocks = state.shape[0]
    group = BW * force_weight.shape[1]
    return pl.pallas_call(
        functools.partial(ocean_kernel, tile_count),
        out_shape=[
            jax.ShapeDtypeStruct(lead1.shape, jnp.bfloat16),
            jax.ShapeDtypeStruct(state.shape, jnp.bfloat16),
        ],
        in_specs=[pl.BlockSpec(memory_space=pltpu.SMEM)] + [vmem] * 7,
        out_specs=[vmem, vmem],
        scratch_shapes=[
            pltpu.VMEM((BH * blocks, 6 * group), jnp.bfloat16),
            pltpu.VMEM((6 * group, 2 * group), jnp.bfloat16),
            pltpu.VMEM((BH * blocks, group), jnp.float32),
        ],
        compiler_params=pltpu.CompilerParams(vmem_limit_bytes=VMEM_LIMIT),
        name="ocean",
    )(rotations, lead1, lead2, state, land, owners, force_weight, gathered)


def local(
    tile_count, atmosphere, ocean_state, land_sea, owners, rotations, conv_weight, conv_bias,
    force_weight, ocean_weight,
):
    joined_ch, ocean_ch = ocean_weight.shape[2:]
    own = ocean_weight[0].reshape(3, 3, joined_ch, ocean_ch)[:, ::-1].transpose(0, 2, 1, 3)
    own = jnp.pad(own, ((0, 0), (0, 0), (0, BW - 3), (0, 0)))
    own = own.reshape(3 * joined_ch, BW * ocean_ch)
    gathered = lax.all_gather(own, "tile", axis=0)
    lead1, lead2 = atmosphere_leads(tile_count, rotations, atmosphere, conv_weight, conv_bias)
    return tuple(
        ocean_step(
            tile_count, rotations, lead1, lead2, ocean_state, land_sea[:, None], owners,
            force_weight, gathered,
        )
    )


def solution(mesh):
    in_specs = (
        P(("ens", "tile"), None, None),
        P(("ens", "tile"), None),
        P("tile"),
        P("tile", None),
        P(),
        P(),
        P(),
        P(),
        P("tile", None, None, None),
    )
    out_specs = (P(("ens", "tile"), None, None), P(("ens", "tile"), None))
    return jax.shard_map(
        functools.partial(local, mesh.shape["tile"]),
        mesh=mesh,
        in_specs=in_specs,
        out_specs=out_specs,
        check_vma=False,
    )
```

```python
import functools
import jax
import jax.numpy as jnp
from jax import lax
from jax.experimental import pallas as pl
from jax.experimental.pallas import tpu as pltpu
from jax.sharding import PartitionSpec as P

LEADS = 2
LAYERS = 3
BH = 4
BW = 4
MARGIN = 2**LAYERS - 1
VMEM_LIMIT = 48 * 1024 * 1024


def one_hot(mask):
    return jnp.where(mask, 1.0, 0.0).astype(jnp.bfloat16)


def moved(matrix, values):
    return jnp.dot(matrix, values, preferred_element_type=jnp.float32).astype(jnp.bfloat16)


def flipped(index, bit):
    return index + (1 - 2 * (index // 2**bit % 2)) * 2**bit


def reversed_bits(index, bits):
    return sum(index // 2**s % 2 * 2 ** (bits - 1 - s) for s in range(bits))


def atmosphere_kernel(
    tile_count, rot_ref, band_ref, w_ref, bias_ref, own_ref, lead1_ref, lead2_ref, v_ref,
    ext, mid1, mid2, taps, send_sem, recv_sem, v_send, v_recv,
):
    me = lax.axis_index("tile")
    rows, columns, channels = band_ref.shape
    has_up = me > 0
    has_down = me < tile_count - 1
    barrier = pltpu.get_barrier_semaphore()
    bits = tile_count.bit_length() - 1
    for s in range(1, bits):
        pl.semaphore_signal(barrier, inc=1, device_id={"tile": flipped(me, s)})

    @pl.when(has_up)
    def _():
        pl.semaphore_signal(barrier, inc=1, device_id={"tile": me - 1})

    @pl.when(has_down)
    def _():
        pl.semaphore_signal(barrier, inc=1, device_id={"tile": me + 1})

    shift = rot_ref[me]
    to = lax.broadcasted_iota(jnp.int32, (columns, columns), 0)
    source = lax.broadcasted_iota(jnp.int32, (columns, columns), 1)
    distance = source - to + shift
    turn = one_hot((distance == 0) | (distance == columns))
    for r in range(rows):
        ext[0, MARGIN + r] = moved(turn, band_ref[r])

    place = reversed_bits(me, bits)
    v_ref[place] = own_ref[...]
    pl.semaphore_wait(
        barrier, bits - 1 + jnp.minimum(me, 1) + jnp.minimum(tile_count - 1 - me, 1)
    )

    def doubling(stage):
        size = 2**stage
        block = v_ref.at[pl.ds(place // size * size, size)]
        return pltpu.make_async_remote_copy(
            src_ref=block,
            dst_ref=block,
            send_sem=v_send.at[stage],
            recv_sem=v_recv.at[stage],
            device_id={"tile": flipped(me, bits - 1 - stage)},
        )

    def advance(stage):
        if 0 < stage <= bits:
            doubling(stage - 1).wait()
        if stage < bits:
            doubling(stage).start()

    def copies(lead):
        up = pltpu.make_async_remote_copy(
            src_ref=ext.at[lead, pl.ds(MARGIN, MARGIN)],
            dst_ref=ext.at[lead, pl.ds(MARGIN + rows, MARGIN)],
            send_sem=send_sem.at[lead, 0],
            recv_sem=recv_sem.at[lead, 0],
            device_id={"tile": me - 1},
        )
        down = pltpu.make_async_remote_copy(
            src_ref=ext.at[lead, pl.ds(rows, MARGIN)],
            dst_ref=ext.at[lead, pl.ds(0, MARGIN)],
            send_sem=send_sem.at[lead, 1],
            recv_sem=recv_sem.at[lead, 1],
            device_id={"tile": me + 1},
        )
        return up, down

    def start(lead):
        up, down = copies(lead)

        @pl.when(has_up)
        def _():
            up.start()

        @pl.when(has_down)
        def _():
            down.start()

    def finish(lead):
        up, down = copies(lead)

        @pl.when(has_up)
        def _():
            down.wait_recv()

        @pl.when(has_down)
        def _():
            up.wait_recv()

    def layer(index, source_of, store, out_rows, margin_left):
        dilation = 2**index
        bias = bias_ref[pl.ds(index, 1), :].astype(jnp.float32)

        def pair(g, carry):
            r = (g // dilation) * (2 * dilation) + g % dilation
            lhs = jnp.concatenate([source_of(r + k * dilation) for k in range(4)], axis=1)
            y = jnp.dot(lhs, taps[index], preferred_element_type=jnp.float32)
            for o in range(2):
                base = o * 3 * channels
                total = (
                    pltpu.roll(y[:, base : base + channels], dilation, 0)
                    + y[:, base + channels : base + 2 * channels]
                    + pltpu.roll(
                        y[:, base + 2 * channels : base + 3 * channels], columns - dilation, 0
                    )
                )
                row = r + o * dilation
                centre = lhs[:, (1 + o) * channels : (2 + o) * channels].astype(jnp.float32)
                value = centre + jax.nn.gelu(total + bias)
                if margin_left:
                    position = me * rows - margin_left + row
                    inside = (position >= 0) & (position < tile_count * rows)
                    value = jnp.where(inside, value, 0.0)
                store(row, value.astype(jnp.bfloat16))
            return carry

        lax.fori_loop(0, out_rows // 2, pair, 0, unroll=2)

    start(0)
    advance(0)
    points = LEADS * LAYERS

    def steps(point):
        for stage in range(1, bits + 1):
            if (stage - 1) * points // bits == point:
                advance(stage)

    for index in range(LAYERS):
        for k in range(4):
            for o in range(2):
                for b in range(3):
                    a = k - o
                    where = (
                        index,
                        pl.ds(k * channels, channels),
                        pl.ds((o * 3 + b) * channels, channels),
                    )
                    if 0 <= a <= 2:
                        taps[where] = w_ref[index, a * 3 + b]
                    else:
                        taps[where] = jnp.zeros((channels, channels), jnp.bfloat16)

    @pl.when(jnp.logical_not(has_up))
    def _():
        for lead in range(LEADS):
            for r in range(MARGIN):
                ext[lead, r] = jnp.zeros((columns, channels), jnp.bfloat16)

    @pl.when(jnp.logical_not(has_down))
    def _():
        for lead in range(LEADS):
            for r in range(MARGIN):
                ext[lead, MARGIN + rows + r] = jnp.zeros((columns, channels), jnp.bfloat16)

    def set_mid1(row, value):
        mid1[row] = value

    def set_mid2(row, value):
        mid2[row] = value

    def set_lead1(row, value):
        lead1_ref[row] = value
        ext[1, MARGIN + row] = value

    def set_lead2(row, value):
        lead2_ref[row] = value

    for lead in range(LEADS):
        finish(lead)
        steps(lead * LAYERS)
        layer(0, lambda r, lead=lead: ext[lead, r], set_mid1, rows + 12, 6)
        steps(lead * LAYERS + 1)
        layer(1, lambda r: mid1[r], set_mid2, rows + 8, 4)
        steps(lead * LAYERS + 2)
        layer(2, lambda r: mid2[r], (set_lead1, set_lead2)[lead], rows, 0)
        if lead + 1 < LEADS:
            start(lead + 1)

    for lead in range(LEADS):
        up, down = copies(lead)

        @pl.when(has_up)
        def _():
            up.wait_send()

        @pl.when(has_down)
        def _():
            down.wait_send()


def atmosphere_leads(tile_count, rotations, band, conv_weight, conv_bias, own):
    rows, columns, channels = band.shape
    vmem = pl.BlockSpec(memory_space=pltpu.VMEM)
    extended = (rows + 2 * MARGIN, columns, channels)
    return pl.pallas_call(
        functools.partial(atmosphere_kernel, tile_count),
        out_shape=[jax.ShapeDtypeStruct(band.shape, jnp.bfloat16)] * 2
        + [jax.ShapeDtypeStruct((tile_count, *own.shape), jnp.bfloat16)],
        in_specs=[pl.BlockSpec(memory_space=pltpu.SMEM)] + [vmem] * 4,
        out_specs=[vmem] * 3,
        scratch_shapes=[
            pltpu.VMEM((LEADS, *extended), jnp.bfloat16),
            pltpu.VMEM((rows + 12, columns, channels), jnp.bfloat16),
            pltpu.VMEM((rows + 8, columns, channels), jnp.bfloat16),
            pltpu.VMEM((LAYERS, 4 * channels, 6 * channels), jnp.bfloat16),
            pltpu.SemaphoreType.DMA((LEADS, 2)),
            pltpu.SemaphoreType.DMA((LEADS, 2)),
            pltpu.SemaphoreType.DMA((tile_count.bit_length() - 1,)),
            pltpu.SemaphoreType.DMA((tile_count.bit_length() - 1,)),
        ],
        compiler_params=pltpu.CompilerParams(
            collective_id=0, has_side_effects=True, vmem_limit_bytes=VMEM_LIMIT
        ),
        cost_estimate=pl.CostEstimate(
            flops=2 * 88 * columns * 9 * channels * channels,
            bytes_accessed=4 * rows * columns * channels * 2,
            transcendentals=88 * columns * channels,
        ),
        name="atmosphere",
    )(rotations, band, conv_weight, conv_bias, own)


def ocean_kernel(
    tile_count, rot_ref, lead1_ref, lead2_ref, state_ref, land_ref, owner_ref, fw_ref, v_ref,
    atmos_ref, sea_ref, lhs, rhs, total,
):
    me = lax.axis_index("tile")
    bits = tile_count.bit_length() - 1
    rows, columns, channels = lead1_ref.shape
    blocks, width = state_ref.shape
    ocean_ch = fw_ref.shape[1]
    cells = BH * BW
    group = BW * ocean_ch
    across = columns // BW
    shift = rot_ref[me]

    to = lax.broadcasted_iota(jnp.int32, (columns, columns), 0)
    source = lax.broadcasted_iota(jnp.int32, (columns, columns), 1)
    distance = to + shift - source
    back = one_hot((distance == 0) | (distance == columns))
    for r in range(rows):
        atmos_ref[r] = moved(back, lead2_ref[r])

    distance = (to % across) * BW + to // across + shift - source
    gather = one_hot((distance == 0) | (distance == columns))
    lane = lax.broadcasted_iota(jnp.int32, (ocean_ch, group), 1)
    spread = one_hot(lane % ocean_ch == lax.broadcasted_iota(jnp.int32, (ocean_ch, group), 0))
    fw4 = moved(fw_ref[...], spread)

    s = lax.broadcasted_iota(jnp.int32, (width, width), 0)
    t = lax.broadcasted_iota(jnp.int32, (width, width), 1)
    permute = one_hot((s // cells == t % ocean_ch) & (s % cells == t // ocean_ch))
    state = moved(state_ref[...], permute)

    piece_lane = lax.broadcasted_iota(jnp.int32, (across, group), 1) // ocean_ch
    lhs[...] = jnp.zeros_like(lhs)
    wide = 2 * group
    for r in range(rows):
        i, pr = r // BH, r % BH
        forcing = 0.5 * (
            jnp.dot(lead1_ref[r], fw4, preferred_element_type=jnp.float32)
            + jnp.dot(lead2_ref[r], fw4, preferred_element_type=jnp.float32)
        )
        y = jnp.dot(gather, forcing.astype(jnp.bfloat16), preferred_element_type=jnp.float32)
        piece = jnp.zeros((across, group), jnp.float32)
        for pc in range(BW):
            piece = jnp.where(piece_lane == pc, y[pc * across : (pc + 1) * across], piece)
        piece = piece.astype(jnp.bfloat16)
        for a in range(3):
            q = pr + 1 - a
            if 0 <= q < BH:
                lhs[pl.ds(q * blocks + i * across, across), pl.ds(a * wide, group)] = piece
    for pr in range(BH):
        for a in range(3):
            q = pr + 1 - a
            if 0 <= q < BH:
                lhs[pl.ds(q * blocks, blocks), pl.ds(a * wide + group, group)] = state[
                    :, pr * group : (pr + 1) * group
                ]

    owner = jnp.concatenate([jnp.broadcast_to(owner_ref[...], (blocks, group))] * BH, axis=0)
    total[...] = jnp.zeros_like(total)
    v_lane = lax.broadcasted_iota(jnp.int32, (v_ref.shape[1], group), 1) // ocean_ch

    def two_owners(k, carry):
        for half in range(2):
            v = v_ref[2 * k + half].astype(jnp.float32)
            for pc in range(BW):
                turned = v if pc == 1 else pltpu.roll(v, ((pc - 1) * ocean_ch) % group, 1)
                if pc == 0:
                    turned = jnp.where(v_lane == BW - 1, 0.0, turned)
                if pc > 2:
                    turned = jnp.where(v_lane < pc - 1, 0.0, turned)
                turned = turned.astype(jnp.bfloat16)
                for ah in range(6):
                    rhs[
                        pl.ds(ah * group + pc * ocean_ch, ocean_ch), pl.ds(half * group, group)
                    ] = turned[ah * ocean_ch : (ah + 1) * ocean_ch]
        y = jnp.dot(lhs[...], rhs[...], preferred_element_type=jnp.float32)
        first = reversed_bits(2 * k, bits)
        kept = jnp.where(owner == first, y[:, :group], total[...])
        total[...] = jnp.where(owner == first + tile_count // 2, y[:, group:], kept)
        return carry

    lax.fori_loop(0, tile_count // 2, two_owners, 0)

    sea = jnp.broadcast_to(land_ref[...], (blocks, group)) > 0
    out = jnp.zeros((blocks, width), jnp.float32)
    t = lax.broadcasted_iota(jnp.int32, (group, width), 0)
    s = lax.broadcasted_iota(jnp.int32, (group, width), 1)
    for q in range(BH):
        old = state[:, q * group : (q + 1) * group].astype(jnp.float32)
        new = old + jax.nn.gelu(total[pl.ds(q * blocks, blocks), :])
        new = jnp.where(sea, new, 0.0).astype(jnp.bfloat16)
        tq = t + q * group
        unpermute = one_hot((s // cells == tq % ocean_ch) & (s % cells == tq // ocean_ch))
        out = out + jnp.dot(new, unpermute, preferred_element_type=jnp.float32)
    sea_ref[...] = out.astype(jnp.bfloat16)


def ocean_step(tile_count, rotations, lead1, lead2, state, land, owners, force_weight, gathered):
    vmem = pl.BlockSpec(memory_space=pltpu.VMEM)
    blocks = state.shape[0]
    group = BW * force_weight.shape[1]
    return pl.pallas_call(
        functools.partial(ocean_kernel, tile_count),
        out_shape=[
            jax.ShapeDtypeStruct(lead1.shape, jnp.bfloat16),
            jax.ShapeDtypeStruct(state.shape, jnp.bfloat16),
        ],
        in_specs=[pl.BlockSpec(memory_space=pltpu.SMEM)] + [vmem] * 7,
        out_specs=[vmem, vmem],
        scratch_shapes=[
            pltpu.VMEM((BH * blocks, 6 * group), jnp.bfloat16),
            pltpu.VMEM((6 * group, 2 * group), jnp.bfloat16),
            pltpu.VMEM((BH * blocks, group), jnp.float32),
        ],
        compiler_params=pltpu.CompilerParams(vmem_limit_bytes=VMEM_LIMIT),
        name="ocean",
    )(rotations, lead1, lead2, state, land, owners, force_weight, gathered)


def local(
    tile_count, atmosphere, ocean_state, land_sea, owners, rotations, conv_weight, conv_bias,
    force_weight, ocean_weight,
):
    joined_ch, ocean_ch = ocean_weight.shape[2:]
    own = ocean_weight[0].reshape(3, 3, joined_ch, ocean_ch)[:, ::-1].transpose(0, 2, 1, 3)
    own = jnp.pad(own, ((0, 0), (0, 0), (0, BW - 3), (0, 0)))
    own = own.reshape(3 * joined_ch, BW * ocean_ch)
    lead1, lead2, gathered = atmosphere_leads(
        tile_count, rotations, atmosphere, conv_weight, conv_bias, own
    )
    return tuple(
        ocean_step(
            tile_count, rotations, lead1, lead2, ocean_state, land_sea[:, None], owners,
            force_weight, gathered,
        )
    )


def solution(mesh):
    in_specs = (
        P(("ens", "tile"), None, None),
        P(("ens", "tile"), None),
        P("tile"),
        P("tile", None),
        P(),
        P(),
        P(),
        P(),
        P("tile", None, None, None),
    )
    out_specs = (P(("ens", "tile"), None, None), P(("ens", "tile"), None))
    return jax.shard_map(
        functools.partial(local, mesh.shape["tile"]),
        mesh=mesh,
        in_specs=in_specs,
        out_specs=out_specs,
        check_vma=False,
    )
```

```python
import functools
import jax
import jax.numpy as jnp
from jax import lax
from jax.experimental import pallas as pl
from jax.experimental.pallas import tpu as pltpu
from jax.sharding import PartitionSpec as P

LEADS = 2
LAYERS = 3
BH = 4
BW = 4
MARGIN = 2**LAYERS - 1
VMEM_LIMIT = 48 * 1024 * 1024


def one_hot(mask):
    return jnp.where(mask, 1.0, 0.0).astype(jnp.bfloat16)


def moved(matrix, values):
    return jnp.dot(matrix, values, preferred_element_type=jnp.float32).astype(jnp.bfloat16)


def flipped(index, bit):
    return index + (1 - 2 * (index // 2**bit % 2)) * 2**bit


def reversed_bits(index, bits):
    return sum(index // 2**s % 2 * 2 ** (bits - 1 - s) for s in range(bits))


GROUPS = ((1, 1), (2, 3), (4, 5), (6, 7))
WAVES = (
    ((0, 6), (0, 12)),
    ((0, 4), (0, 14), (1, 4), (1, 5), (1, 8), (1, 9)),
    ((0, 2), (0, 16)),
    ((0, 0), (0, 18), (1, 0), (1, 1), (1, 12), (1, 13)),
)
INTERIOR = ((0, 8), (0, 10))


def atmosphere_kernel(
    tile_count, rot_ref, band_ref, w_ref, bias_ref, ow_ref, leads_ref, v_ref,
    ext, mid1, mid2, taps, send_sem, recv_sem, v_send, v_recv,
):
    me = lax.axis_index("tile")
    rows, columns, channels = band_ref.shape
    has_up = me > 0
    has_down = me < tile_count - 1
    barrier = pltpu.get_barrier_semaphore()
    bits = tile_count.bit_length() - 1
    for s in range(1, bits):
        pl.semaphore_signal(barrier, inc=1, device_id={"tile": flipped(me, s)})

    @pl.when(has_up)
    def _():
        pl.semaphore_signal(barrier, inc=1, device_id={"tile": me - 1})

    @pl.when(has_down)
    def _():
        pl.semaphore_signal(barrier, inc=1, device_id={"tile": me + 1})

    shift = rot_ref[me]
    to = lax.broadcasted_iota(jnp.int32, (columns, columns), 0)
    source = lax.broadcasted_iota(jnp.int32, (columns, columns), 1)
    distance = source - to + shift
    turn = one_hot((distance == 0) | (distance == columns))

    def turn_rows(*which):
        for r in which:
            ext[0, MARGIN + r] = moved(turn, band_ref[r])

    def up_copy(lead, group):
        near, far = GROUPS[group]
        return pltpu.make_async_remote_copy(
            src_ref=ext.at[lead, pl.ds(MARGIN + near - 1, far - near + 1)],
            dst_ref=ext.at[lead, pl.ds(MARGIN + rows + near - 1, far - near + 1)],
            send_sem=send_sem.at[lead, 0, group],
            recv_sem=recv_sem.at[lead, 0, group],
            device_id={"tile": me - 1},
        )

    def down_copy(lead, group):
        near, far = GROUPS[group]
        return pltpu.make_async_remote_copy(
            src_ref=ext.at[lead, pl.ds(MARGIN + rows - far, far - near + 1)],
            dst_ref=ext.at[lead, pl.ds(MARGIN - far, far - near + 1)],
            send_sem=send_sem.at[lead, 1, group],
            recv_sem=recv_sem.at[lead, 1, group],
            device_id={"tile": me + 1},
        )

    def start(lead, *groups, also=True):
        @pl.when(has_up & also)
        def _():
            for group in groups:
                up_copy(lead, group).start()

        @pl.when(has_down & also)
        def _():
            for group in groups:
                down_copy(lead, group).start()

    def arrive(lead, group):
        @pl.when(has_up)
        def _():
            down_copy(lead, group).wait_recv()

        @pl.when(has_down)
        def _():
            up_copy(lead, group).wait_recv()

    place = reversed_bits(me, bits)

    def doubling(stage):
        size = 2**stage
        block = v_ref.at[pl.ds(place // size * size, size)]
        return pltpu.make_async_remote_copy(
            src_ref=block,
            dst_ref=block,
            send_sem=v_send.at[stage],
            recv_sem=v_recv.at[stage],
            device_id={"tile": flipped(me, bits - 1 - stage)},
        )

    def advance(stage):
        if 0 < stage <= bits:
            doubling(stage - 1).wait()
        if stage < bits:
            doubling(stage).start()

    def pair(lead, index, r):
        dilation = 2**index
        margin_left = (6, 4, 0)[index]
        bias = bias_ref[index : index + 1, :].astype(jnp.float32)
        field = (ext.at[lead], mid1, mid2)[index]
        lhs = jnp.concatenate([field[r + k * dilation] for k in range(4)], axis=1)
        y = jnp.dot(lhs, taps[index], preferred_element_type=jnp.float32)
        for o in range(2):
            base = o * 3 * channels
            sums = (
                pltpu.roll(y[:, base : base + channels], dilation, 0)
                + y[:, base + channels : base + 2 * channels]
                + pltpu.roll(
                    y[:, base + 2 * channels : base + 3 * channels], columns - dilation, 0
                )
            )
            row = r + o * dilation
            centre = lhs[:, (1 + o) * channels : (2 + o) * channels].astype(jnp.float32)
            value = centre + jax.nn.gelu(sums + bias)
            if row < margin_left or row >= margin_left + rows:
                value = jnp.where(has_up if row < margin_left else has_down, value, 0.0)
            value = value.astype(jnp.bfloat16)
            if index == 0:
                mid1[row] = value
            elif index == 1:
                mid2[row] = value
            else:
                leads_ref[lead, row] = value
                ext[lead + 1, MARGIN + row] = value

    turn_rows(0, rows - 1)
    pl.semaphore_wait(
        barrier, bits - 1 + jnp.minimum(me, 1) + jnp.minimum(tile_count - 1 - me, 1)
    )
    start(0, 0)
    turn_rows(1, 2, 5, 6)
    start(0, 1)
    turn_rows(3, 4)
    start(0, 2, 3)

    for a in range(3):
        parts = [ow_ref[a * 3 + b].astype(jnp.float32) for b in (2, 1, 0)]
        parts = jnp.concatenate(parts + [jnp.zeros_like(parts[0])], axis=0)
        v_ref[place, pl.ds(a * parts.shape[1], parts.shape[1]), :] = parts.T.astype(jnp.bfloat16)
    advance(0)

    for index in range(LAYERS):
        for k in range(4):
            for o in range(2):
                for b in range(3):
                    a = k - o
                    where = (
                        index,
                        pl.ds(k * channels, channels),
                        pl.ds((o * 3 + b) * channels, channels),
                    )
                    if 0 <= a <= 2:
                        taps[where] = w_ref[index, a * 3 + b]
                    else:
                        taps[where] = jnp.zeros((channels, channels), jnp.bfloat16)

    @pl.when(jnp.logical_not(has_up))
    def _():
        for lead in range(LEADS):
            for r in range(MARGIN):
                ext[lead, r] = jnp.zeros((columns, channels), jnp.bfloat16)

    @pl.when(jnp.logical_not(has_down))
    def _():
        for lead in range(LEADS):
            for r in range(MARGIN):
                ext[lead, MARGIN + rows + r] = jnp.zeros((columns, channels), jnp.bfloat16)

    points = LEADS * len(GROUPS)

    def one_lead(lead, carry):
        for index, r in INTERIOR:
            pair(lead, index, r)
        for group in range(len(GROUPS)):
            arrive(lead, group)
            for stage in range(1, bits + 1):
                point = (stage - 1) * points // bits
                if point % len(GROUPS) == group:

                    @pl.when(lead == point // len(GROUPS))
                    def _(stage=stage):
                        advance(stage)

            for index, r in WAVES[group]:
                pair(lead, index, r)
        more = lead + 1 < LEADS
        pair(lead, 2, 0)
        pair(lead, 2, 3)
        start(lead + 1, 0, also=more)
        pair(lead, 2, 1)
        pair(lead, 2, 2)
        start(lead + 1, 1, 2, 3, also=more)
        return carry

    lax.fori_loop(0, LEADS, one_lead, 0)

    for lead in range(LEADS):

        @pl.when(has_up)
        def _(lead=lead):
            for group in range(len(GROUPS)):
                up_copy(lead, group).wait_send()

        @pl.when(has_down)
        def _(lead=lead):
            for group in range(len(GROUPS)):
                down_copy(lead, group).wait_send()


def atmosphere_leads(tile_count, rotations, band, conv_weight, conv_bias, ocean_weight):
    rows, columns, channels = band.shape
    vmem = pl.BlockSpec(memory_space=pltpu.VMEM)
    extended = (rows + 2 * MARGIN, columns, channels)
    ocean_ch, joined_ch = ocean_weight.shape[1:]
    gathered = (tile_count, 3 * joined_ch, BW * ocean_ch)
    return pl.pallas_call(
        functools.partial(atmosphere_kernel, tile_count),
        out_shape=[
            jax.ShapeDtypeStruct((LEADS, *band.shape), jnp.bfloat16),
            jax.ShapeDtypeStruct(gathered, jnp.bfloat16),
        ],
        in_specs=[pl.BlockSpec(memory_space=pltpu.SMEM)] + [vmem] * 4,
        out_specs=[vmem] * 2,
        scratch_shapes=[
            pltpu.VMEM((LEADS + 1, *extended), jnp.bfloat16),
            pltpu.VMEM((rows + 12, columns, channels), jnp.bfloat16),
            pltpu.VMEM((rows + 8, columns, channels), jnp.bfloat16),
            pltpu.VMEM((LAYERS, 4 * channels, 6 * channels), jnp.bfloat16),
            pltpu.SemaphoreType.DMA((LEADS, 2, len(GROUPS))),
            pltpu.SemaphoreType.DMA((LEADS, 2, len(GROUPS))),
            pltpu.SemaphoreType.DMA((tile_count.bit_length() - 1,)),
            pltpu.SemaphoreType.DMA((tile_count.bit_length() - 1,)),
        ],
        compiler_params=pltpu.CompilerParams(
            collective_id=0, has_side_effects=True, vmem_limit_bytes=VMEM_LIMIT
        ),
        cost_estimate=pl.CostEstimate(
            flops=2 * 88 * columns * 9 * channels * channels,
            bytes_accessed=4 * rows * columns * channels * 2,
            transcendentals=88 * columns * channels,
        ),
        name="atmosphere",
    )(rotations, band, conv_weight, conv_bias, ocean_weight)


def ocean_kernel(
    tile_count, rot_ref, leads_ref, state_ref, land_ref, owner_ref, fw_ref, v_ref,
    atmos_ref, sea_ref, lhs, rhs, total,
):
    me = lax.axis_index("tile")
    bits = tile_count.bit_length() - 1
    rows, columns, channels = leads_ref.shape[1:]
    blocks, width = state_ref.shape
    ocean_ch = fw_ref.shape[0]
    cells = BH * BW
    group = BW * ocean_ch
    across = columns // BW
    shift = rot_ref[me]

    to = lax.broadcasted_iota(jnp.int32, (columns, columns), 0)
    source = lax.broadcasted_iota(jnp.int32, (columns, columns), 1)
    distance = to + shift - source
    back = one_hot((distance == 0) | (distance == columns))
    for r in range(rows):
        atmos_ref[r] = moved(back, leads_ref[1, r])

    distance = (to % across) * BW + to // across + shift - source
    gather = one_hot((distance == 0) | (distance == columns))
    fw4 = jnp.concatenate([fw_ref[...].astype(jnp.float32)] * BW, axis=0).T.astype(jnp.bfloat16)

    s = lax.broadcasted_iota(jnp.int32, (width, width), 0)
    t = lax.broadcasted_iota(jnp.int32, (width, width), 1)
    permute = one_hot((s // cells == t % ocean_ch) & (s % cells == t // ocean_ch))
    state = moved(state_ref[...], permute)

    piece_lane = lax.broadcasted_iota(jnp.int32, (across, group), 1) // ocean_ch
    lhs[...] = jnp.zeros_like(lhs)
    wide = 2 * group
    for r in range(rows):
        i, pr = r // BH, r % BH
        forcing = 0.5 * (
            jnp.dot(leads_ref[0, r], fw4, preferred_element_type=jnp.float32)
            + jnp.dot(leads_ref[1, r], fw4, preferred_element_type=jnp.float32)
        )
        y = jnp.dot(gather, forcing.astype(jnp.bfloat16), preferred_element_type=jnp.float32)
        piece = jnp.zeros((across, group), jnp.float32)
        for pc in range(BW):
            piece = jnp.where(piece_lane == pc, y[pc * across : (pc + 1) * across], piece)
        piece = piece.astype(jnp.bfloat16)
        for a in range(3):
            q = pr + 1 - a
            if 0 <= q < BH:
                lhs[pl.ds(q * blocks + i * across, across), pl.ds(a * wide, group)] = piece
    for pr in range(BH):
        for a in range(3):
            q = pr + 1 - a
            if 0 <= q < BH:
                lhs[pl.ds(q * blocks, blocks), pl.ds(a * wide + group, group)] = state[
                    :, pr * group : (pr + 1) * group
                ]

    owner = jnp.broadcast_to(owner_ref[...].astype(jnp.float32), (group, blocks)).T
    owner = jnp.concatenate([owner] * BH, axis=0)
    total[...] = jnp.zeros_like(total)
    v_lane = lax.broadcasted_iota(jnp.int32, (v_ref.shape[1], group), 1) // ocean_ch

    def two_owners(k, carry):
        for half in range(2):
            v = v_ref[2 * k + half].astype(jnp.float32)
            for pc in range(BW):
                turned = v if pc == 1 else pltpu.roll(v, ((pc - 1) * ocean_ch) % group, 1)
                if pc == 0:
                    turned = jnp.where(v_lane == BW - 1, 0.0, turned)
                if pc > 2:
                    turned = jnp.where(v_lane < pc - 1, 0.0, turned)
                turned = turned.astype(jnp.bfloat16)
                for ah in range(6):
                    rhs[
                        pl.ds(ah * group + pc * ocean_ch, ocean_ch), pl.ds(half * group, group)
                    ] = turned[ah * ocean_ch : (ah + 1) * ocean_ch]
        y = jnp.dot(lhs[...], rhs[...], preferred_element_type=jnp.float32)
        first = reversed_bits(2 * k, bits).astype(jnp.float32)
        kept = jnp.where(owner == first, y[:, :group], total[...])
        total[...] = jnp.where(owner == first + tile_count // 2, y[:, group:], kept)
        return carry

    lax.fori_loop(0, tile_count // 2, two_owners, 0)

    sea = jnp.broadcast_to(land_ref[...].astype(jnp.float32), (group, blocks)).T > 0
    out = jnp.zeros((blocks, width), jnp.float32)
    t = lax.broadcasted_iota(jnp.int32, (group, width), 0)
    s = lax.broadcasted_iota(jnp.int32, (group, width), 1)
    for q in range(BH):
        old = state[:, q * group : (q + 1) * group].astype(jnp.float32)
        new = old + jax.nn.gelu(total[pl.ds(q * blocks, blocks), :])
        new = jnp.where(sea, new, 0.0).astype(jnp.bfloat16)
        tq = t + q * group
        unpermute = one_hot((s // cells == tq % ocean_ch) & (s % cells == tq // ocean_ch))
        out = out + jnp.dot(new, unpermute, preferred_element_type=jnp.float32)
    sea_ref[...] = out.astype(jnp.bfloat16)


def ocean_step(tile_count, rotations, leads, state, land, owners, force_weight, gathered):
    vmem = pl.BlockSpec(memory_space=pltpu.VMEM)
    blocks = state.shape[0]
    group = BW * force_weight.shape[0]
    return pl.pallas_call(
        functools.partial(ocean_kernel, tile_count),
        out_shape=[
            jax.ShapeDtypeStruct(leads.shape[1:], jnp.bfloat16),
            jax.ShapeDtypeStruct(state.shape, jnp.bfloat16),
        ],
        in_specs=[pl.BlockSpec(memory_space=pltpu.SMEM)] + [vmem] * 6,
        out_specs=[vmem, vmem],
        scratch_shapes=[
            pltpu.VMEM((BH * blocks, 6 * group), jnp.bfloat16),
            pltpu.VMEM((6 * group, 2 * group), jnp.bfloat16),
            pltpu.VMEM((BH * blocks, group), jnp.float32),
        ],
        compiler_params=pltpu.CompilerParams(vmem_limit_bytes=VMEM_LIMIT),
        name="ocean",
    )(rotations, leads, state, land, owners, force_weight, gathered)


def local(
    tile_count, atmosphere, ocean_state, land_sea, owners, rotations, conv_weight, conv_bias,
    force_weight, ocean_weight,
):
    leads, gathered = atmosphere_leads(
        tile_count, rotations, atmosphere, conv_weight, conv_bias,
        ocean_weight[0].transpose(0, 2, 1),
    )
    return tuple(
        ocean_step(
            tile_count, rotations, leads, ocean_state, land_sea[None, :], owners.T,
            force_weight.T, gathered,
        )
    )


def solution(mesh):
    in_specs = (
        P(("ens", "tile"), None, None),
        P(("ens", "tile"), None),
        P("tile"),
        P("tile", None),
        P(),
        P(),
        P(),
        P(),
        P("tile", None, None, None),
    )
    out_specs = (P(("ens", "tile"), None, None), P(("ens", "tile"), None))
    return jax.shard_map(
        functools.partial(local, mesh.shape["tile"]),
        mesh=mesh,
        in_specs=in_specs,
        out_specs=out_specs,
        check_vma=False,
    )
```
